32 devices in a mesh: grp: 2 (over x), long: 16 (over z, y, core).
Axes of the slice: x: 2, y: 2, z: 4, core: 2. Of those that a mesh axis runs over, the one named last changes fastest.
Arguments:
- pixel_map: int32 [256, 2048], P(('grp', 'long')), parts along dimension 0, may hold values from 0 to 3
- materials: float32 [8], P('grp'), parts along dimension 0, may hold values from 1.5 to 12
- mode_panel: float32 [128, 2, 201, 201], P(('grp', 'long')), parts along dimension 0, may hold values from -1.6 to 1.6
Outputs:
- coupled_panel: float32 [128, 2, 201, 201], P(('grp', 'long')), parts along dimension 0
The draws below stay inside these ranges and needn't reach their ends.
There are 2 independent parts, one for each index of `grp`. The reference program is written for one: setup_inputs(seed, part) draws one part's arguments, and reference() takes and returns one part's arrays. A program takes and returns all parts, laid end to end along the dimension named above; each array names one. Nothing has to cross between parts.
All inputs are finite; a program needn't handle non-finite values.
Results may differ from the reference program's by a relative error of at most 0.0003.
Values sent between devices are 32-bit elements; how exact they have to be, the bound alone decides.
A program may use at most 128 MiB of HBM per device.

```python
import math
import jax
import jax.numpy as jnp
from jax import lax

NPIX = 2048
ORD = 201
YORD = 201
COLS = 64
NMAT = 4
NS_ITERS = 3
LINES = 128


def draw_pixel_map(key, part):
    first_key, second_key = jax.random.split(jax.random.fold_in(key, 11))
    edges = jax.random.randint(first_key, (LINES, NPIX), 0, 16)
    starts = (edges == 0).astype(jnp.int32)
    segment = jnp.cumsum(starts, axis=1).astype(jnp.int32)
    labels = jax.random.randint(second_key, (LINES, NPIX + 1), 0, NMAT)
    return jnp.take_along_axis(labels, segment, axis=1).astype(jnp.int32)


def steps_of(stream_key, shape, pieces, low, high):
    def one(position, parts):
        steps = jax.random.uniform(jax.random.fold_in(jax.random.fold_in(stream_key, 6), position), (parts,), jnp.float32, low / len(pieces), high / len(pieces))
        return jnp.repeat(jnp.exp(steps), shape[position] // parts).reshape((-1,) + (1,) * (len(shape) - position - 1))

    loudness = one(*pieces[0])
    for cut in pieces[1:]:
        loudness = loudness * one(*cut)
    return loudness


def scatter_about(stream_key, dims, spread, limit, cuts=(), kind=jnp.bfloat16):
    result = jax.random.normal(stream_key, dims, jnp.float32) * spread
    if len(cuts) > 0:
        result = steps_of(stream_key, dims, cuts, -0.22, 0.18) * result
    return jnp.clip(result, min=-limit, max=limit).astype(kind)


def setup_inputs(seed: int = 0, part: int = 0) -> dict:
    keys = jax.random.split(jax.random.key(seed), 4)
    own_keys = jax.random.split(jax.random.fold_in(keys[3], part), 4)
    pixel_map = draw_pixel_map(jax.random.fold_in(jax.random.fold_in(keys[3], part), 71), part)
    materials = jnp.clip(jax.random.uniform(own_keys[1], (NMAT,), jnp.float32, 1.5, 12.0), 1.5, 12.0)
    mode_panel = scatter_about(own_keys[2], (COLS, 2, YORD, ORD), 0.2, 1.6, ((0, 16),), jnp.float32)
    return dict(pixel_map=pixel_map, materials=materials, mode_panel=mode_panel)


exact_mode = lax.Precision.HIGHEST


def phase_table(first, second, period):
    turns = jnp.mod(first[:, None] * second[None, :], period)
    angle = turns.astype(jnp.float32) * (2.0 * math.pi / period)
    return jnp.cos(angle), jnp.sin(angle)


def complex_product(left_real, left_imag, right_real, right_imag):
    real = jnp.einsum("lmk,lkn->lmn", left_real, right_real, precision=exact_mode) - jnp.einsum("lmk,lkn->lmn", left_imag, right_imag, precision=exact_mode)
    imag = jnp.einsum("lmk,lkn->lmn", left_real, right_imag, precision=exact_mode) + jnp.einsum("lmk,lkn->lmn", left_imag, right_real, precision=exact_mode)
    return real, imag


def line_inverse(pixel_rows, materials):
    inverse_eps = jnp.zeros(pixel_rows.shape, jnp.float32)
    for material in range(NMAT):
        inverse_eps = inverse_eps + jnp.where(pixel_rows == material, 1.0 / materials[material], 0.0)
    orders = jnp.arange(2 * ORD - 1, dtype=jnp.int32) - (ORD - 1)
    pixels = jnp.arange(NPIX, dtype=jnp.int32)
    cosine, sine = phase_table(orders, pixels, NPIX)
    coef_real = jnp.einsum("lx,kx->lk", inverse_eps, cosine, precision=exact_mode) / NPIX
    coef_imag = -jnp.einsum("lx,kx->lk", inverse_eps, sine, precision=exact_mode) / NPIX
    offsets = (jnp.arange(ORD, dtype=jnp.int32)[:, None] - jnp.arange(ORD, dtype=jnp.int32)[None, :] + (ORD - 1)).astype(jnp.int32)
    toep_real = coef_real[:, offsets]
    toep_imag = coef_imag[:, offsets]
    factor = 2.0 / (1.0 / jnp.min(materials) + 1.0 / jnp.max(materials))
    identity = jnp.eye(ORD, dtype=jnp.float32)
    iterate_real = 2.0 * factor * identity - factor * factor * toep_real
    iterate_imag = -factor * factor * toep_imag
    for sweep in range(NS_ITERS - 1):
        inner_real, inner_imag = complex_product(toep_real, toep_imag, iterate_real, iterate_imag)
        outer_real, outer_imag = complex_product(iterate_real, iterate_imag, inner_real, inner_imag)
        iterate_real = 2.0 * iterate_real - outer_real
        iterate_imag = 2.0 * iterate_imag - outer_imag
    return iterate_real, iterate_imag


def reference(pixel_map, materials, mode_panel):
    inverse_real, inverse_imag = line_inverse(pixel_map, materials)
    lines = pixel_map.shape[0]
    half = (YORD - 1) // 2
    line_ids = jnp.arange(lines, dtype=jnp.int32)
    y_orders = jnp.arange(YORD, dtype=jnp.int32) - half
    cosine, sine = phase_table(line_ids, y_orders, lines)
    panel_real = mode_panel[:, 0]
    panel_imag = mode_panel[:, 1]
    spread_real = jnp.einsum("yp,cpn->cyn", cosine, panel_real, precision=exact_mode) - jnp.einsum("yp,cpn->cyn", sine, panel_imag, precision=exact_mode)
    spread_imag = jnp.einsum("yp,cpn->cyn", cosine, panel_imag, precision=exact_mode) + jnp.einsum("yp,cpn->cyn", sine, panel_real, precision=exact_mode)
    applied_real = jnp.einsum("ymn,cyn->cym", inverse_real, spread_real, precision=exact_mode) - jnp.einsum("ymn,cyn->cym", inverse_imag, spread_imag, precision=exact_mode)
    applied_imag = jnp.einsum("ymn,cyn->cym", inverse_real, spread_imag, precision=exact_mode) + jnp.einsum("ymn,cyn->cym", inverse_imag, spread_real, precision=exact_mode)
    out_real = (jnp.einsum("yp,cym->cpm", cosine, applied_real, precision=exact_mode) + jnp.einsum("yp,cym->cpm", sine, applied_imag, precision=exact_mode)) / lines
    out_imag = (jnp.einsum("yp,cym->cpm", cosine, applied_imag, precision=exact_mode) - jnp.einsum("yp,cym->cpm", sine, applied_real, precision=exact_mode)) / lines
    return jnp.stack([out_real, out_imag], axis=1)
```

```python
import functools

import jax
import jax.numpy as jnp
import ml_dtypes
import numpy as np
from jax import lax
from jax.experimental import pallas as pl
from jax.experimental.pallas import tpu as pltpu
from jax.sharding import PartitionSpec as P

NS_ITERS = 3
BLOCK = 128
VMEM_BYTES = 56 * 1024 * 1024


def round_up(value, step):
    return -(-value // step) * step


def split_table(table):
    high = table.astype(np.float32).astype(ml_dtypes.bfloat16)
    low = (table - high.astype(np.float64)).astype(ml_dtypes.bfloat16)
    return high, low


def turns(first, second, period):
    return np.mod(np.outer(first, second), period) * (2.0 * np.pi / period)


def symbol_table(orders, pixels):
    reach = orders - 1
    period = 2 * orders - 1
    lanes = round_up(orders, 2 * BLOCK)
    harmonics = np.arange(1, reach + 1)
    frequencies = np.arange(orders)
    by_frequency = turns(harmonics, frequencies, period)
    by_pixel = turns(np.arange(pixels), harmonics, pixels)
    table = np.zeros((pixels, 2 * lanes))
    table[:, :orders] = (1.0 + 2.0 * np.cos(by_pixel) @ np.cos(by_frequency)) / pixels
    table[:, lanes : lanes + orders] = -2.0 * np.sin(by_pixel) @ np.sin(by_frequency) / pixels
    return split_table(table)


def order_tables(orders):
    period = 2 * orders - 1
    lanes = round_up(orders, 2 * BLOCK)
    angle = turns(np.arange(orders) - (orders - 1) // 2, np.arange(orders), period)
    weight = np.where(np.arange(orders) == 0, 1.0, 2.0)[:, None] / period
    forward = np.zeros((lanes, 2 * lanes))
    forward[:orders, :orders] = np.cos(angle)
    forward[:orders, lanes : lanes + orders] = np.sin(angle)
    backward = np.zeros((2 * lanes, lanes))
    backward[:orders, :orders] = weight * np.cos(angle).T
    backward[lanes : lanes + orders, :orders] = weight * np.sin(angle).T
    even = backward[:lanes] @ forward[:, :lanes]
    odd = backward[lanes:] @ forward[:, lanes:]
    return split_table(forward), split_table(backward), split_table(even), split_table(odd)


def line_tables(y_orders, lines):
    kept = min(y_orders, lines)
    padded = round_up(kept, BLOCK)
    blocks = lines // BLOCK
    angle = turns(np.arange(lines), np.arange(kept) - (y_orders - 1) // 2, lines)
    cosine = np.zeros((blocks, BLOCK, padded))
    sine = np.zeros((blocks, BLOCK, padded))
    cosine[:, :, :kept] = np.cos(angle).reshape(blocks, BLOCK, kept)
    sine[:, :, :kept] = np.sin(angle).reshape(blocks, BLOCK, kept)
    real = np.concatenate([cosine, -sine], axis=2)
    imag = np.concatenate([sine, cosine], axis=2)
    spread = np.stack([real, imag], axis=1).reshape(2 * lines, 2 * padded)
    return split_table(spread), split_table(spread.T / lines)


def split(value):
    high = value.astype(jnp.bfloat16)
    return high, (value - high.astype(jnp.float32)).astype(jnp.bfloat16)


def mul(left, right):
    return jnp.dot(left, right, preferred_element_type=jnp.float32)


def mul_table(high, low, table_high, table_low):
    return mul(high, table_high) + mul(low, table_high) + mul(high, table_low)


def scale_of(materials, shape):
    values = [jnp.full(shape, materials[i], jnp.float32) for i in range(materials.shape[0])]
    least = functools.reduce(jnp.minimum, values)
    most = functools.reduce(jnp.maximum, values)
    return 2.0 / (1.0 / least + 1.0 / most)


def symbol_kernel(materials, pixel_rows, table_high, table_low, symbol):
    pixels = pixel_rows[...]
    count = pixels.shape[0]
    inverse_eps = jnp.zeros(pixels.shape, jnp.float32)
    for i in range(materials.shape[0]):
        inverse = 1.0 / jnp.full(pixels.shape, materials[i], jnp.float32)
        inverse_eps = jnp.where(pixels == i, inverse, inverse_eps)
    high, low = split(inverse_eps)
    rows = jnp.concatenate([high, low], axis=0)
    sums = mul(rows, table_high[...]) + mul(rows, table_low[...])
    sums = sums[:count] + sums[count:]
    lanes = sums.shape[1] // 2
    scaled = scale_of(materials, sums.shape) * sums
    symbol[:, :lanes] = 1.0 - scaled[:, :lanes]
    symbol[:, lanes:] = -scaled[:, lanes:]


def panel_kernel(
    materials,
    panel,
    symbol,
    spread_high,
    spread_low,
    gather_high,
    gather_low,
    forward_high,
    forward_low,
    backward_high,
    backward_low,
    even_high,
    even_low,
    odd_high,
    odd_low,
    out,
    folded,
    spread,
    start,
    state,
    high_side,
    low_side,
):
    columns, _, y_orders, orders = panel.shape
    lines, width = symbol.shape
    lanes = width // 2
    blocks = lines // BLOCK
    unit = 2 * BLOCK
    units = columns * blocks
    group = 2 if units % 2 == 0 else 1
    kept = min(y_orders, lines)
    padded = spread_high.shape[1] // 2

    folded[...] = jnp.zeros(folded.shape, jnp.float32)
    for c in range(columns):
        for part in range(2):
            base = part * padded
            folded[c, base : base + kept, :orders] = panel[c, part, :kept, :]
            for first in range(kept, y_orders, kept):
                size = min(kept, y_orders - first)
                folded[c, base : base + size, :orders] += panel[c, part, first : first + size, :]
        high, low = split(folded[c])
        spread[c * 2 * lines : (c + 1) * 2 * lines, :] = (
            mul(spread_high[...], high) + mul(spread_high[...], low) + mul(spread_low[...], high)
        )

    for g in range(0, units, group):
        rows = slice(g * unit, (g + group) * unit)
        high, low = split(spread[rows, :])
        value = mul_table(high, low, forward_high[...], forward_low[...])
        start[rows, :] = value
        state[rows, :] = value

    def weigh(u):
        real = slice(u * unit, u * unit + BLOCK)
        imag = slice(u * unit + BLOCK, (u + 1) * unit)
        here = slice((u % blocks) * BLOCK, (u % blocks + 1) * BLOCK)
        p = symbol[here, :lanes]
        q = symbol[here, lanes:]
        even_real = state[real, :lanes]
        even_imag = state[imag, :lanes]
        odd_real = state[real, lanes:]
        odd_imag = state[imag, lanes:]
        for rows, cols, value in (
            (real, slice(0, lanes), p * even_real + q * odd_imag),
            (imag, slice(0, lanes), p * even_imag - q * odd_real),
            (real, slice(lanes, width), p * odd_real - q * even_imag),
            (imag, slice(lanes, width), p * odd_imag + q * even_real),
        ):
            high, low = split(value)
            high_side[rows, cols] = high
            low_side[rows, cols] = low

    def sweep(_, carry):
        for g in range(0, units, group):
            rows = slice(g * unit, (g + group) * unit)
            for u in range(g, g + group):
                weigh(u)
            state[rows, :lanes] = start[rows, :lanes] + mul_table(
                high_side[rows, :lanes], low_side[rows, :lanes], even_high[...], even_low[...]
            )
            state[rows, lanes:] = start[rows, lanes:] + mul_table(
                high_side[rows, lanes:], low_side[rows, lanes:], odd_high[...], odd_low[...]
            )
        return carry

    lax.fori_loop(0, 2**NS_ITERS - 2, sweep, 0)

    scale = scale_of(materials, (1, lanes))
    for g in range(0, units, group):
        rows = slice(g * unit, (g + group) * unit)
        for u in range(g, g + group):
            weigh(u)
        spread[rows, :] = scale * (
            spread[rows, :]
            + mul_table(high_side[rows, :], low_side[rows, :], backward_high[...], backward_low[...])
        )

    for c in range(columns):
        high, low = split(spread[c * 2 * lines : (c + 1) * 2 * lines, :])
        value = (
            mul(gather_high[...], high) + mul(gather_high[...], low) + mul(gather_low[...], high)
        )
        for part in range(2):
            base = part * padded
            for first in range(0, y_orders, kept):
                size = min(kept, y_orders - first)
                out[c, part, first : first + size, :] = value[base : base + size, :orders]


def whole(count):
    return [pl.BlockSpec(memory_space=pltpu.VMEM)] * count


def local(pixel_map, materials, mode_panel):
    rows, pixels = pixel_map.shape
    columns, _, y_orders, orders = mode_panel.shape
    lines = rows * lax.axis_size("long")
    lanes = round_up(orders, 2 * BLOCK)
    width = 2 * lanes
    scalars = pl.BlockSpec(memory_space=pltpu.SMEM)
    params = pltpu.CompilerParams(vmem_limit_bytes=VMEM_BYTES)
    symbol = pl.pallas_call(
        symbol_kernel,
        out_shape=jax.ShapeDtypeStruct((rows, width), jnp.float32),
        in_specs=[scalars] + whole(3),
        out_specs=pl.BlockSpec(memory_space=pltpu.VMEM),
        compiler_params=params,
        name="symbol",
    )(materials, pixel_map, *map(jnp.asarray, symbol_table(orders, pixels)))
    symbol = lax.all_gather(symbol, "long", axis=0, tiled=True)
    spread_table, gather_table = line_tables(y_orders, lines)
    forward, backward, even, odd = order_tables(orders)
    tables = [*spread_table, *gather_table, *forward, *backward, *even, *odd]
    total = columns * 2 * lines
    folded_rows = spread_table[0].shape[1]
    return pl.pallas_call(
        panel_kernel,
        out_shape=jax.ShapeDtypeStruct(mode_panel.shape, jnp.float32),
        in_specs=[scalars] + whole(2 + len(tables)),
        out_specs=pl.BlockSpec(memory_space=pltpu.VMEM),
        scratch_shapes=[
            pltpu.VMEM((columns, folded_rows, lanes), jnp.float32),
            pltpu.VMEM((total, lanes), jnp.float32),
            pltpu.VMEM((total, width), jnp.float32),
            pltpu.VMEM((total, width), jnp.float32),
            pltpu.VMEM((total, width), jnp.bfloat16),
            pltpu.VMEM((total, width), jnp.bfloat16),
        ],
        compiler_params=params,
        name="panel",
    )(materials, mode_panel, symbol, *map(jnp.asarray, tables))


def solution(mesh):
    in_specs = (P(("grp", "long"), None), P("grp"), P(("grp", "long"), None, None, None))
    out_specs = P(("grp", "long"), None, None, None)
    return jax.shard_map(local, mesh=mesh, in_specs=in_specs, out_specs=out_specs, check_vma=False)
```

```python
import functools

import jax
import jax.numpy as jnp
import ml_dtypes
import numpy as np
from jax import lax
from jax.experimental import pallas as pl
from jax.experimental.pallas import tpu as pltpu
from jax.sharding import PartitionSpec as P

NS_ITERS = 3
BLOCK = 128
CHUNKS = 4
VMEM_BYTES = 28 * 1024 * 1024


def round_up(value, step):
    return -(-value // step) * step


def split_table(table):
    high = table.astype(np.float32).astype(ml_dtypes.bfloat16)
    low = (table - high.astype(np.float64)).astype(ml_dtypes.bfloat16)
    return high, low


def turns(first, second, period):
    return np.mod(np.outer(first, second), period) * (2.0 * np.pi / period)


def symbol_table(orders, pixels):
    reach = orders - 1
    period = 2 * orders - 1
    lanes = round_up(orders, 2 * BLOCK)
    harmonics = np.arange(1, reach + 1)
    frequencies = np.arange(orders)
    by_frequency = turns(harmonics, frequencies, period)
    by_pixel = turns(np.arange(pixels), harmonics, pixels)
    table = np.zeros((pixels, 2 * lanes))
    table[:, :orders] = (1.0 + 2.0 * np.cos(by_pixel) @ np.cos(by_frequency)) / pixels
    table[:, lanes : lanes + orders] = -2.0 * np.sin(by_pixel) @ np.sin(by_frequency) / pixels
    return split_table(table)


def order_tables(orders):
    period = 2 * orders - 1
    lanes = round_up(orders, 2 * BLOCK)
    angle = turns(np.arange(orders) - (orders - 1) // 2, np.arange(orders), period)
    weight = np.where(np.arange(orders) == 0, 1.0, 2.0)[:, None] / period
    forward = np.zeros((lanes, 2 * lanes))
    forward[:orders, :orders] = np.cos(angle)
    forward[:orders, lanes : lanes + orders] = np.sin(angle)
    backward = np.zeros((2 * lanes, lanes))
    backward[:orders, :orders] = weight * np.cos(angle).T
    backward[lanes : lanes + orders, :orders] = weight * np.sin(angle).T
    even = backward[:lanes] @ forward[:, :lanes]
    odd = backward[lanes:] @ forward[:, lanes:]
    return split_table(forward), split_table(backward), split_table(even), split_table(odd)


def line_tables(y_orders, lines):
    kept = min(y_orders, lines)
    padded = round_up(kept, BLOCK)
    blocks = lines // BLOCK
    angle = turns(np.arange(lines), np.arange(kept) - (y_orders - 1) // 2, lines)
    cosine = np.zeros((blocks, BLOCK, padded))
    sine = np.zeros((blocks, BLOCK, padded))
    cosine[:, :, :kept] = np.cos(angle).reshape(blocks, BLOCK, kept)
    sine[:, :, :kept] = np.sin(angle).reshape(blocks, BLOCK, kept)
    real = np.concatenate([cosine, -sine], axis=2)
    imag = np.concatenate([sine, cosine], axis=2)
    spread = np.stack([real, imag], axis=1).reshape(2 * lines, 2 * padded)
    return split_table(spread), split_table(spread.T / lines)


def split(value):
    high = value.astype(jnp.bfloat16)
    return high, (value - high.astype(jnp.float32)).astype(jnp.bfloat16)


def mul(left, right):
    return jnp.dot(left, right, preferred_element_type=jnp.float32)


def mul_table(high, low, table_high, table_low):
    return mul(high, table_high) + mul(low, table_high) + mul(high, table_low)


def scale_of(materials, shape):
    values = [jnp.full(shape, materials[i], jnp.float32) for i in range(materials.shape[0])]
    least = functools.reduce(jnp.minimum, values)
    most = functools.reduce(jnp.maximum, values)
    return 2.0 / (1.0 / least + 1.0 / most)


def symbol_of(materials, pixels, tables, fetched, sums):
    inverse_eps = jnp.zeros(pixels.shape, jnp.float32)
    for i in range(materials.shape[0]):
        inverse = 1.0 / jnp.full(pixels.shape, materials[i], jnp.float32)
        inverse_eps = jnp.where(pixels == i, inverse, inverse_eps)
    high, low = split(inverse_eps)
    rows = jnp.concatenate([high, low], axis=0)
    count = pixels.shape[0]
    total = jnp.zeros((2 * count, tables[0].shape[1]), jnp.float32)
    depth = rows.shape[1] // len(fetched)
    for i, copies in enumerate(fetched):
        part = slice(i * depth, (i + 1) * depth)
        for copy, table in zip(copies, tables):
            copy.wait()
            total += mul(rows[:, part], table[part, :])
    total = total[:count] + total[count:]
    lanes = total.shape[1] // 2
    scaled = scale_of(materials, total.shape) * total
    sums[:, :lanes] = 1.0 - scaled[:, :lanes]
    sums[:, lanes:] = -scaled[:, lanes:]


def gather_kernel(
    materials,
    pixel_rows,
    panel,
    spread_high,
    spread_low,
    forward_high,
    forward_low,
    table_high,
    table_low,
    symbol,
    spread,
    start,
    high_table,
    low_table,
    landed,
    folded,
    fetch_sem,
    send_sem,
    recv_sem,
):
    me = lax.axis_index("long")
    devices = lax.axis_size("long")
    barrier = pltpu.get_barrier_semaphore()
    for i in range(1, devices):
        pl.semaphore_signal(barrier, inc=1, device_id={"long": lax.rem(me + i, devices)})
    pixels = pixel_rows[...]
    depth = table_high.shape[0] // CHUNKS
    fetched = []
    for i in range(CHUNKS):
        part = pl.ds(i * depth, depth)
        copies = [
            pltpu.make_async_copy(source.at[part], target.at[part], fetch_sem.at[2 * i + j])
            for j, (source, target) in enumerate(((table_high, high_table), (table_low, low_table)))
        ]
        for copy in copies:
            copy.start()
        fetched.append(copies)
    count = pixels.shape[0]
    mine = landed.at[pl.ds(pl.multiple_of(me * count, count), count)]
    symbol_of(materials, pixels, (high_table, low_table), fetched, mine)
    pl.semaphore_wait(barrier, devices - 1)
    sent = []
    for i in range(1, devices):
        copy = pltpu.make_async_remote_copy(
            src_ref=mine,
            dst_ref=mine,
            send_sem=send_sem.at[i],
            recv_sem=recv_sem.at[i],
            device_id={"long": lax.rem(me + i, devices)},
        )
        copy.start()
        sent.append(copy)

    columns, y_orders, _, orders = panel.shape
    lines = symbol.shape[0]
    kept = min(y_orders, lines)
    padded = spread_high.shape[1] // 2
    folded[...] = jnp.zeros(folded.shape, jnp.float32)
    for c in range(columns):
        for part in range(2):
            base = part * padded
            folded[c, base : base + kept, :orders] = panel[c, :kept, part, :]
            for first in range(kept, y_orders, kept):
                size = min(kept, y_orders - first)
                folded[c, base : base + size, :orders] += panel[c, first : first + size, part, :]
        high, low = split(folded[c])
        value = (
            mul(spread_high[...], high) + mul(spread_high[...], low) + mul(spread_low[...], high)
        )
        rows = slice(c * 2 * lines, (c + 1) * 2 * lines)
        spread[rows, :] = value
        high, low = split(value)
        start[rows, :] = mul_table(high, low, forward_high[...], forward_low[...])

    for copy in sent:
        copy.wait()
    symbol[...] = landed[...]


def panel_kernel(
    materials,
    symbol,
    spread,
    start,
    gather_high,
    gather_low,
    backward_high,
    backward_low,
    even_high,
    even_low,
    odd_high,
    odd_low,
    out,
    state,
    high_side,
    low_side,
):
    columns, y_orders, _, orders = out.shape
    lines, width = symbol.shape
    lanes = width // 2
    blocks = lines // BLOCK
    unit = 2 * BLOCK
    units = columns * blocks
    group = 2 if units % 2 == 0 else 1
    kept = min(y_orders, lines)
    padded = gather_high.shape[0] // 2

    def weigh(u, state):
        real = slice(u * unit, u * unit + BLOCK)
        imag = slice(u * unit + BLOCK, (u + 1) * unit)
        here = slice((u % blocks) * BLOCK, (u % blocks + 1) * BLOCK)
        p = symbol[here, :lanes]
        q = symbol[here, lanes:]
        even_real = state[real, :lanes]
        even_imag = state[imag, :lanes]
        odd_real = state[real, lanes:]
        odd_imag = state[imag, lanes:]
        for rows, cols, value in (
            (real, slice(0, lanes), p * even_real + q * odd_imag),
            (imag, slice(0, lanes), p * even_imag - q * odd_real),
            (real, slice(lanes, width), p * odd_real - q * even_imag),
            (imag, slice(lanes, width), p * odd_imag + q * even_real),
        ):
            high, low = split(value)
            high_side[rows, cols] = high
            low_side[rows, cols] = low

    def sweep(source):
        for g in range(0, units, group):
            rows = slice(g * unit, (g + group) * unit)
            for u in range(g, g + group):
                weigh(u, source)
            state[rows, :lanes] = start[rows, :lanes] + mul_table(
                high_side[rows, :lanes], low_side[rows, :lanes], even_high[...], even_low[...]
            )
            state[rows, lanes:] = start[rows, lanes:] + mul_table(
                high_side[rows, lanes:], low_side[rows, lanes:], odd_high[...], odd_low[...]
            )

    sweep(start)

    def again(_, carry):
        sweep(state)
        return carry

    lax.fori_loop(0, 2**NS_ITERS - 3, again, 0)

    scale = scale_of(materials, (1, lanes))
    for g in range(0, units, group):
        rows = slice(g * unit, (g + group) * unit)
        for u in range(g, g + group):
            weigh(u, state)
        state[rows, :lanes] = scale * (
            spread[rows, :]
            + mul_table(high_side[rows, :], low_side[rows, :], backward_high[...], backward_low[...])
        )

    for c in range(columns):
        high, low = split(state[c * 2 * lines : (c + 1) * 2 * lines, :lanes])
        value = (
            mul(gather_high[...], high) + mul(gather_high[...], low) + mul(gather_low[...], high)
        )
        for part in range(2):
            base = part * padded
            for first in range(0, y_orders, kept):
                size = min(kept, y_orders - first)
                out[c, first : first + size, part, :] = value[base : base + size, :orders]


def whole(count):
    return [pl.BlockSpec(memory_space=pltpu.VMEM)] * count


def local(pixel_map, materials, mode_panel):
    rows, pixels = pixel_map.shape
    columns, _, y_orders, orders = mode_panel.shape
    devices = lax.axis_size("long")
    lines = rows * devices
    lanes = round_up(orders, 2 * BLOCK)
    width = 2 * lanes
    total = columns * 2 * lines
    scalars = pl.BlockSpec(memory_space=pltpu.SMEM)
    symbol_pair = symbol_table(orders, pixels)
    spread_pair, gather_pair = line_tables(y_orders, lines)
    forward, backward, even, odd = order_tables(orders)
    tables = [*spread_pair, *forward]
    panel = mode_panel.transpose(0, 2, 1, 3)
    symbol, spread, start = pl.pallas_call(
        gather_kernel,
        out_shape=[
            jax.ShapeDtypeStruct((lines, width), jnp.float32),
            jax.ShapeDtypeStruct((total, lanes), jnp.float32),
            jax.ShapeDtypeStruct((total, width), jnp.float32),
        ],
        in_specs=[scalars] + whole(2 + len(tables)) + [pl.BlockSpec(memory_space=pl.ANY)] * 2,
        out_specs=whole(3),
        scratch_shapes=[
            pltpu.VMEM((pixels, width), jnp.bfloat16),
            pltpu.VMEM((pixels, width), jnp.bfloat16),
            pltpu.VMEM((lines, width), jnp.float32),
            pltpu.VMEM((columns, spread_pair[0].shape[1], lanes), jnp.float32),
            pltpu.SemaphoreType.DMA((2 * CHUNKS,)),
            pltpu.SemaphoreType.DMA((devices,)),
            pltpu.SemaphoreType.DMA((devices,)),
        ],
        compiler_params=pltpu.CompilerParams(
            vmem_limit_bytes=VMEM_BYTES, collective_id=0, has_side_effects=True
        ),
        name="gather",
    )(materials, pixel_map, panel, *map(jnp.asarray, tables), *map(jnp.asarray, symbol_pair))
    tables = [*gather_pair, *backward, *even, *odd]
    result = pl.pallas_call(
        panel_kernel,
        out_shape=jax.ShapeDtypeStruct(panel.shape, jnp.float32),
        in_specs=[scalars] + whole(3 + len(tables)),
        out_specs=pl.BlockSpec(memory_space=pltpu.VMEM),
        scratch_shapes=[
            pltpu.VMEM((total, width), jnp.float32),
            pltpu.VMEM((total, width), jnp.bfloat16),
            pltpu.VMEM((total, width), jnp.bfloat16),
        ],
        compiler_params=pltpu.CompilerParams(vmem_limit_bytes=VMEM_BYTES),
        name="panel",
    )(materials, symbol, spread, start, *map(jnp.asarray, tables))
    return result.transpose(0, 2, 1, 3)


def solution(mesh):
    in_specs = (P(("grp", "long"), None), P("grp"), P(("grp", "long"), None, None, None))
    out_specs = P(("grp", "long"), None, None, None)
    return jax.shard_map(local, mesh=mesh, in_specs=in_specs, out_specs=out_specs, check_vma=False)
```

```python
import functools

import jax
import jax.numpy as jnp
import ml_dtypes
import numpy as np
from jax import lax
from jax.experimental import pallas as pl
from jax.experimental.pallas import tpu as pltpu
from jax.sharding import PartitionSpec as P

NS_ITERS = 3
BLOCK = 128
CHUNKS = 4
VMEM_BYTES = 62 * 1024 * 1024


def round_up(value, step):
    return -(-value // step) * step


def split_table(table):
    high = table.astype(np.float32).astype(ml_dtypes.bfloat16)
    low = (table - high.astype(np.float64)).astype(ml_dtypes.bfloat16)
    return high, low


def turns(first, second, period):
    return np.mod(np.outer(first, second), period) * (2.0 * np.pi / period)


def symbol_table(orders, pixels):
    reach = orders - 1
    period = 2 * orders - 1
    lanes = round_up(orders, 2 * BLOCK)
    harmonics = np.arange(1, reach + 1)
    frequencies = np.arange(orders)
    by_frequency = turns(harmonics, frequencies, period)
    by_pixel = turns(np.arange(pixels), harmonics, pixels)
    table = np.zeros((pixels, 2 * lanes))
    table[:, :orders] = (1.0 + 2.0 * np.cos(by_pixel) @ np.cos(by_frequency)) / pixels
    table[:, lanes : lanes + orders] = -2.0 * np.sin(by_pixel) @ np.sin(by_frequency) / pixels
    return split_table(table)


def order_tables(orders):
    period = 2 * orders - 1
    lanes = round_up(orders, 2 * BLOCK)
    angle = turns(np.arange(orders) - (orders - 1) // 2, np.arange(orders), period)
    weight = np.where(np.arange(orders) == 0, 1.0, 2.0)[:, None] / period
    forward = np.zeros((lanes, 2 * lanes))
    forward[:orders, :orders] = np.cos(angle)
    forward[:orders, lanes : lanes + orders] = np.sin(angle)
    backward = np.zeros((2 * lanes, lanes))
    backward[:orders, :orders] = weight * np.cos(angle).T
    backward[lanes : lanes + orders, :orders] = weight * np.sin(angle).T
    even = backward[:lanes] @ forward[:, :lanes]
    odd = backward[lanes:] @ forward[:, lanes:]
    return split_table(forward), split_table(backward), split_table(even), split_table(odd)


def line_tables(y_orders, lines):
    kept = min(y_orders, lines)
    padded = round_up(kept, BLOCK)
    blocks = lines // BLOCK
    angle = turns(np.arange(lines), np.arange(kept) - (y_orders - 1) // 2, lines)
    cosine = np.zeros((blocks, BLOCK, padded))
    sine = np.zeros((blocks, BLOCK, padded))
    cosine[:, :, :kept] = np.cos(angle).reshape(blocks, BLOCK, kept)
    sine[:, :, :kept] = np.sin(angle).reshape(blocks, BLOCK, kept)
    real = np.concatenate([cosine, -sine], axis=2)
    imag = np.concatenate([sine, cosine], axis=2)
    spread = np.stack([real, imag], axis=1).reshape(2 * lines, 2 * padded)
    return split_table(spread), split_table(spread.T / lines)


def split(value):
    high = value.astype(jnp.bfloat16)
    return high, (value - high.astype(jnp.float32)).astype(jnp.bfloat16)


def mul(left, right):
    return jnp.dot(left, right, preferred_element_type=jnp.float32)


def mul_table(high, low, table_high, table_low):
    return mul(high, table_high) + mul(low, table_high) + mul(high, table_low)


def scale_of(materials, shape):
    values = [jnp.full(shape, materials[i], jnp.float32) for i in range(materials.shape[0])]
    least = functools.reduce(jnp.minimum, values)
    most = functools.reduce(jnp.maximum, values)
    return 2.0 / (1.0 / least + 1.0 / most)


def symbol_of(materials, pixels, tables, fetched, sums):
    inverse_eps = jnp.zeros(pixels.shape, jnp.float32)
    for i in range(materials.shape[0]):
        inverse = 1.0 / jnp.full(pixels.shape, materials[i], jnp.float32)
        inverse_eps = jnp.where(pixels == i, inverse, inverse_eps)
    high, low = split(inverse_eps)
    rows = jnp.concatenate([high, low], axis=0)
    count = pixels.shape[0]
    total = jnp.zeros((2 * count, tables[0].shape[1]), jnp.float32)
    depth = rows.shape[1] // len(fetched)
    for i, copies in enumerate(fetched):
        part = slice(i * depth, (i + 1) * depth)
        for copy, table in zip(copies, tables):
            copy.wait()
            total += mul(rows[:, part], table[part, :])
    total = total[:count] + total[count:]
    lanes = total.shape[1] // 2
    scaled = scale_of(materials, total.shape) * total
    sums[:, :lanes] = 1.0 - scaled[:, :lanes]
    sums[:, lanes:] = -scaled[:, lanes:]


def apply_kernel(
    materials,
    pixel_rows,
    panel,
    spread_high,
    spread_low,
    forward_high,
    forward_low,
    gather_high_far,
    gather_low_far,
    backward_high_far,
    backward_low_far,
    even_high_far,
    even_low_far,
    odd_high_far,
    odd_low_far,
    table_high,
    table_low,
    out,
    scalars,
    pixels,
    panel_here,
    spread_high_here,
    spread_low_here,
    forward_high_here,
    forward_low_here,
    gather_high,
    gather_low,
    backward_high,
    backward_low,
    even_high,
    even_low,
    odd_high,
    odd_low,
    high_table,
    low_table,
    landed,
    folded,
    spread,
    start,
    state,
    high_side,
    low_side,
    result,
    fetch_sem,
    send_sem,
    recv_sem,
    store_sem,
):
    sources = (
        (materials, scalars),
        (pixel_rows, pixels),
        (panel, panel_here),
        (spread_high, spread_high_here),
        (spread_low, spread_low_here),
        (forward_high, forward_high_here),
        (forward_low, forward_low_here),
        (gather_high_far, gather_high),
        (gather_low_far, gather_low),
        (backward_high_far, backward_high),
        (backward_low_far, backward_low),
        (even_high_far, even_high),
        (even_low_far, even_low),
        (odd_high_far, odd_high),
        (odd_low_far, odd_low),
    )
    fetches = [
        pltpu.make_async_copy(source, target, fetch_sem.at[2 * CHUNKS + i])
        for i, (source, target) in enumerate(sources)
    ]
    early, late = fetches[:7], fetches[7:]
    for copy in early[:2]:
        copy.start()
    me = lax.axis_index("long")
    devices = lax.axis_size("long")
    barrier = pltpu.get_barrier_semaphore()
    for i in range(1, devices):
        pl.semaphore_signal(barrier, inc=1, device_id={"long": lax.rem(me + i, devices)})
    depth = table_high.shape[0] // CHUNKS
    fetched = []
    for i in range(CHUNKS):
        part = pl.ds(i * depth, depth)
        copies = [
            pltpu.make_async_copy(source.at[part], target.at[part], fetch_sem.at[2 * i + j])
            for j, (source, target) in enumerate(((table_high, high_table), (table_low, low_table)))
        ]
        for copy in copies:
            copy.start()
        fetched.append(copies)
    for copy in early[2:] + late:
        copy.start()
    count = pixels.shape[0]
    mine = landed.at[pl.ds(pl.multiple_of(me * count, count), count)]
    for copy in early[:2]:
        copy.wait()
    symbol_of(scalars, pixels[...], (high_table, low_table), fetched, mine)
    pl.semaphore_wait(barrier, devices - 1)
    sent = []
    for i in range(1, devices):
        copy = pltpu.make_async_remote_copy(
            src_ref=mine,
            dst_ref=mine,
            send_sem=send_sem.at[i],
            recv_sem=recv_sem.at[i],
            device_id={"long": lax.rem(me + i, devices)},
        )
        copy.start()
        sent.append(copy)

    columns, y_orders, _, orders = panel.shape
    lines = landed.shape[0]
    kept = min(y_orders, lines)
    padded = spread_high.shape[1] // 2
    folded[...] = jnp.zeros(folded.shape, jnp.float32)
    for copy in early[2:]:
        copy.wait()
    for c in range(columns):
        for part in range(2):
            base = part * padded
            folded[c, base : base + kept, :orders] = panel_here[c, :kept, part, :]
            for first in range(kept, y_orders, kept):
                size = min(kept, y_orders - first)
                folded[c, base : base + size, :orders] += panel_here[c, first : first + size, part, :]
        high, low = split(folded[c])
        value = (
            mul(spread_high_here[...], high)
            + mul(spread_high_here[...], low)
            + mul(spread_low_here[...], high)
        )
        rows = slice(c * 2 * lines, (c + 1) * 2 * lines)
        spread[rows, :] = value
        high, low = split(value)
        start[rows, :] = mul_table(high, low, forward_high_here[...], forward_low_here[...])

    for copy in sent:
        copy.wait()
    symbol = landed
    for copy in late:
        copy.wait()

    width = symbol.shape[1]
    lanes = width // 2
    blocks = lines // BLOCK
    unit = 2 * BLOCK
    units = columns * blocks
    group = 2 if units % 2 == 0 else 1
    kept = min(y_orders, lines)
    padded = gather_high.shape[0] // 2

    def weigh(u, state):
        real = slice(u * unit, u * unit + BLOCK)
        imag = slice(u * unit + BLOCK, (u + 1) * unit)
        here = slice((u % blocks) * BLOCK, (u % blocks + 1) * BLOCK)
        p = symbol[here, :lanes]
        q = symbol[here, lanes:]
        even_real = state[real, :lanes]
        even_imag = state[imag, :lanes]
        odd_real = state[real, lanes:]
        odd_imag = state[imag, lanes:]
        for rows, cols, value in (
            (real, slice(0, lanes), p * even_real + q * odd_imag),
            (imag, slice(0, lanes), p * even_imag - q * odd_real),
            (real, slice(lanes, width), p * odd_real - q * even_imag),
            (imag, slice(lanes, width), p * odd_imag + q * even_real),
        ):
            high, low = split(value)
            high_side[rows, cols] = high
            low_side[rows, cols] = low

    def sweep(source):
        for g in range(0, units, group):
            rows = slice(g * unit, (g + group) * unit)
            for u in range(g, g + group):
                weigh(u, source)
            state[rows, :lanes] = start[rows, :lanes] + mul_table(
                high_side[rows, :lanes], low_side[rows, :lanes], even_high[...], even_low[...]
            )
            state[rows, lanes:] = start[rows, lanes:] + mul_table(
                high_side[rows, lanes:], low_side[rows, lanes:], odd_high[...], odd_low[...]
            )

    for i in range(2**NS_ITERS - 2):
        sweep(state if i else start)

    scale = scale_of(scalars, (1, lanes))
    for g in range(0, units, group):
        rows = slice(g * unit, (g + group) * unit)
        for u in range(g, g + group):
            weigh(u, state)
        state[rows, :lanes] = scale * (
            spread[rows, :]
            + mul_table(high_side[rows, :], low_side[rows, :], backward_high[...], backward_low[...])
        )

    stores = []
    for c in range(columns):
        high, low = split(state[c * 2 * lines : (c + 1) * 2 * lines, :lanes])
        value = (
            mul(gather_high[...], high) + mul(gather_high[...], low) + mul(gather_low[...], high)
        )
        for part in range(2):
            base = part * padded
            for first in range(0, y_orders, kept):
                size = min(kept, y_orders - first)
                result[c, first : first + size, part, :] = value[base : base + size, :orders]
        stores.append(pltpu.make_async_copy(result.at[c], out.at[c], store_sem.at[c]))
        stores[-1].start()
    for store in stores:
        store.wait()


def local(pixel_map, materials, mode_panel):
    rows, pixels = pixel_map.shape
    columns, _, y_orders, orders = mode_panel.shape
    devices = lax.axis_size("long")
    lines = rows * devices
    lanes = round_up(orders, 2 * BLOCK)
    width = 2 * lanes
    total = columns * 2 * lines
    symbol_pair = symbol_table(orders, pixels)
    spread_pair, gather_pair = line_tables(y_orders, lines)
    forward, backward, even, odd = order_tables(orders)
    tables = [*spread_pair, *forward, *gather_pair, *backward, *even, *odd]
    panel = mode_panel.transpose(0, 2, 1, 3)
    result = pl.pallas_call(
        apply_kernel,
        out_shape=jax.ShapeDtypeStruct(panel.shape, jnp.float32),
        in_specs=[pl.BlockSpec(memory_space=pl.ANY)] * (5 + len(tables)),
        out_specs=pl.BlockSpec(memory_space=pl.ANY),
        scratch_shapes=[
            pltpu.SMEM(materials.shape, jnp.float32),
            pltpu.VMEM(pixel_map.shape, jnp.int32),
            pltpu.VMEM(panel.shape, jnp.float32),
            *[pltpu.VMEM(table.shape, jnp.bfloat16) for table in tables],
            pltpu.VMEM((pixels, width), jnp.bfloat16),
            pltpu.VMEM((pixels, width), jnp.bfloat16),
            pltpu.VMEM((lines, width), jnp.float32),
            pltpu.VMEM((columns, spread_pair[0].shape[1], lanes), jnp.float32),
            pltpu.VMEM((total, lanes), jnp.float32),
            pltpu.VMEM((total, width), jnp.float32),
            pltpu.VMEM((total, width), jnp.float32),
            pltpu.VMEM((total, width), jnp.bfloat16),
            pltpu.VMEM((total, width), jnp.bfloat16),
            pltpu.VMEM(panel.shape, jnp.float32),
            pltpu.SemaphoreType.DMA((2 * CHUNKS + 3 + len(tables),)),
            pltpu.SemaphoreType.DMA((devices,)),
            pltpu.SemaphoreType.DMA((devices,)),
            pltpu.SemaphoreType.DMA((columns,)),
        ],
        compiler_params=pltpu.CompilerParams(
            vmem_limit_bytes=VMEM_BYTES, collective_id=0, has_side_effects=True
        ),
        name="apply",
    )(materials, pixel_map, panel, *map(jnp.asarray, tables), *map(jnp.asarray, symbol_pair))
    return result.transpose(0, 2, 1, 3)


def solution(mesh):
    in_specs = (P(("grp", "long"), None), P("grp"), P(("grp", "long"), None, None, None))
    out_specs = P(("grp", "long"), None, None, None)
    return jax.shard_map(local, mesh=mesh, in_specs=in_specs, out_specs=out_specs, check_vma=False)
```

```python
import functools

import jax
import jax.numpy as jnp
import ml_dtypes
import numpy as np
from jax import lax
from jax.experimental import pallas as pl
from jax.experimental.pallas import tpu as pltpu
from jax.sharding import PartitionSpec as P

NS_ITERS = 3
BLOCK = 128
CHUNKS = 4
VMEM_BYTES = 62 * 1024 * 1024


def round_up(value, step):
    return -(-value // step) * step


def split_table(table):
    high = table.astype(np.float32).astype(ml_dtypes.bfloat16)
    low = (table - high.astype(np.float64)).astype(ml_dtypes.bfloat16)
    return high, low


def turns(first, second, period):
    return np.mod(np.outer(first, second), period) * (2.0 * np.pi / period)


def symbol_table(orders, pixels):
    reach = orders - 1
    period = 2 * orders - 1
    lanes = round_up(orders, 2 * BLOCK)
    harmonics = np.arange(1, reach + 1)
    frequencies = np.arange(orders)
    by_frequency = turns(harmonics, frequencies, period)
    by_pixel = turns(np.arange(pixels), harmonics, pixels)
    table = np.zeros((pixels, 2 * lanes))
    table[:, :orders] = (1.0 + 2.0 * np.cos(by_pixel) @ np.cos(by_frequency)) / pixels
    table[:, lanes : lanes + orders] = -2.0 * np.sin(by_pixel) @ np.sin(by_frequency) / pixels
    return split_table(table)


def order_tables(orders):
    period = 2 * orders - 1
    lanes = round_up(orders, 2 * BLOCK)
    angle = turns(np.arange(orders) - (orders - 1) // 2, np.arange(orders), period)
    weight = np.where(np.arange(orders) == 0, 1.0, 2.0)[:, None] / period
    forward = np.zeros((lanes, 2 * lanes))
    forward[:orders, :orders] = np.cos(angle)
    forward[:orders, lanes : lanes + orders] = np.sin(angle)
    backward = np.zeros((2 * lanes, lanes))
    backward[:orders, :orders] = weight * np.cos(angle).T
    backward[lanes : lanes + orders, :orders] = weight * np.sin(angle).T
    even = backward[:lanes] @ forward[:, :lanes]
    odd = backward[lanes:] @ forward[:, lanes:]
    return split_table(forward), split_table(backward), split_table(even), split_table(odd)


def line_tables(y_orders, lines):
    kept = min(y_orders, lines)
    padded = round_up(kept, BLOCK)
    blocks = lines // BLOCK
    angle = turns(np.arange(lines), np.arange(kept) - (y_orders - 1) // 2, lines)
    cosine = np.zeros((blocks, BLOCK, padded))
    sine = np.zeros((blocks, BLOCK, padded))
    cosine[:, :, :kept] = np.cos(angle).reshape(blocks, BLOCK, kept)
    sine[:, :, :kept] = np.sin(angle).reshape(blocks, BLOCK, kept)
    real = np.concatenate([cosine, -sine], axis=2)
    imag = np.concatenate([sine, cosine], axis=2)
    spread = np.stack([real, imag], axis=1).reshape(2 * lines, 2 * padded)
    return split_table(spread), split_table(spread.T / lines)


def split(value):
    high = value.astype(jnp.bfloat16)
    return high, (value - high.astype(jnp.float32)).astype(jnp.bfloat16)


def mul(left, right):
    return jnp.dot(left, right, preferred_element_type=jnp.float32)


def mul_table(high, low, table_high, table_low):
    return mul(high, table_high) + mul(low, table_high) + mul(high, table_low)


def scale_of(materials, shape):
    values = [jnp.full(shape, materials[i], jnp.float32) for i in range(materials.shape[0])]
    least = functools.reduce(jnp.minimum, values)
    most = functools.reduce(jnp.maximum, values)
    return 2.0 / (1.0 / least + 1.0 / most)


def symbol_of(materials, pixels, tables, fetched, sums):
    inverse_eps = jnp.zeros(pixels.shape, jnp.float32)
    for i in range(materials.shape[0]):
        inverse = 1.0 / jnp.full(pixels.shape, materials[i], jnp.float32)
        inverse_eps = jnp.where(pixels == i, inverse, inverse_eps)
    high, low = split(inverse_eps)
    rows = jnp.concatenate([high, low], axis=0)
    count = pixels.shape[0]
    total = jnp.zeros((2 * count, tables[0].shape[1]), jnp.float32)
    depth = rows.shape[1] // len(fetched)
    for i, copies in enumerate(fetched):
        part = slice(i * depth, (i + 1) * depth)
        for copy, table in zip(copies, tables):
            copy.wait()
            total += mul(rows[:, part], table[part, :])
    total = total[:count] + total[count:]
    lanes = total.shape[1] // 2
    scaled = scale_of(materials, total.shape) * total
    sums[:, :lanes] = 1.0 - scaled[:, :lanes]
    sums[:, lanes:] = -scaled[:, lanes:]


def apply_kernel(
    materials,
    pixel_rows,
    panel,
    spread_high,
    spread_low,
    forward_high,
    forward_low,
    backward_high_far,
    backward_low_far,
    even_high_far,
    even_low_far,
    odd_high_far,
    odd_low_far,
    table_high,
    table_low,
    out,
    scalars,
    pixels,
    panel_here,
    spread_high_here,
    spread_low_here,
    forward_high_here,
    forward_low_here,
    backward_high,
    backward_low,
    even_high,
    even_low,
    odd_high,
    odd_low,
    high_table,
    low_table,
    landed,
    folded,
    spread,
    start,
    state,
    high_side,
    low_side,
    fetch_sem,
    send_sem,
    recv_sem,
    store_sem,
):
    sources = (
        (materials, scalars),
        (pixel_rows, pixels),
        (panel, panel_here),
        (spread_high, spread_high_here),
        (spread_low, spread_low_here),
        (forward_high, forward_high_here),
        (forward_low, forward_low_here),
        (backward_high_far, backward_high),
        (backward_low_far, backward_low),
        (even_high_far, even_high),
        (even_low_far, even_low),
        (odd_high_far, odd_high),
        (odd_low_far, odd_low),
    )
    fetches = [
        pltpu.make_async_copy(source, target, fetch_sem.at[2 * CHUNKS + i])
        for i, (source, target) in enumerate(sources)
    ]
    early, late = fetches[:7], fetches[7:]
    for copy in early[:2]:
        copy.start()
    me = lax.axis_index("long")
    devices = lax.axis_size("long")
    cores = 2
    chips = devices // cores
    chip = me // cores
    core = lax.rem(me, cores)
    sibling = chip * cores + (1 - core)

    def twin(i):
        return lax.rem(chip + i, chips) * cores + core

    barrier = pltpu.get_barrier_semaphore()
    for peer in [sibling] + [twin(i) for i in range(1, chips)]:
        pl.semaphore_signal(barrier, inc=1, device_id={"long": peer})
    depth = table_high.shape[0] // CHUNKS
    fetched = []
    for i in range(CHUNKS):
        part = pl.ds(i * depth, depth)
        copies = [
            pltpu.make_async_copy(source.at[part], target.at[part], fetch_sem.at[2 * i + j])
            for j, (source, target) in enumerate(((table_high, high_table), (table_low, low_table)))
        ]
        for copy in copies:
            copy.start()
        fetched.append(copies)
    for copy in early[2:] + late:
        copy.start()
    count = pixels.shape[0]

    def slot(device):
        return landed.at[pl.ds(pl.multiple_of(device * count, count), count)]

    def send(device, peer, i):
        return pltpu.make_async_remote_copy(
            src_ref=slot(device),
            dst_ref=slot(device),
            send_sem=send_sem.at[i],
            recv_sem=recv_sem.at[i],
            device_id={"long": peer},
        )

    mine = slot(me)
    for copy in early[:2]:
        copy.wait()
    symbol_of(scalars, pixels[...], (high_table, low_table), fetched, mine)
    pl.semaphore_wait(barrier, chips)
    sent = [send(me, twin(i), i) for i in range(1, chips)]
    handed = [send(me, sibling, chips)]
    for copy in sent[::-1] + handed:
        copy.start()

    def hand_on():
        for i in range(1, chips):
            sent[i - 1].wait()
            handed.append(send(twin(chips - i), sibling, chips + i))
            handed[-1].start()

    columns, y_orders, _, orders = panel.shape
    lines = landed.shape[0]
    kept = min(y_orders, lines)
    padded = spread_high.shape[1] // 2
    folded[...] = jnp.zeros(folded.shape, jnp.float32)
    for copy in early[2:]:
        copy.wait()
    for c in range(columns):
        for part in range(2):
            base = part * padded
            folded[c, base : base + kept, :orders] = panel_here[c, :kept, part, :]
            for first in range(kept, y_orders, kept):
                size = min(kept, y_orders - first)
                folded[c, base : base + size, :orders] += panel_here[c, first : first + size, part, :]
        high, low = split(folded[c])
        value = (
            mul(spread_high_here[...], high)
            + mul(spread_high_here[...], low)
            + mul(spread_low_here[...], high)
        )
        rows = slice(c * 2 * lines, (c + 1) * 2 * lines)
        spread[rows, :] = value
        high, low = split(value)
        start[rows, :] = mul_table(high, low, forward_high_here[...], forward_low_here[...])
        if c == max(columns - 2, 0):
            hand_on()

    for copy in handed:
        copy.wait()
    symbol = landed
    for copy in late:
        copy.wait()

    width = symbol.shape[1]
    lanes = width // 2
    blocks = lines // BLOCK
    unit = 2 * BLOCK
    units = columns * blocks
    group = 2 if units % 2 == 0 else 1

    def weigh(u, state):
        real = slice(u * unit, u * unit + BLOCK)
        imag = slice(u * unit + BLOCK, (u + 1) * unit)
        here = slice((u % blocks) * BLOCK, (u % blocks + 1) * BLOCK)
        p = symbol[here, :lanes]
        q = symbol[here, lanes:]
        even_real = state[real, :lanes]
        even_imag = state[imag, :lanes]
        odd_real = state[real, lanes:]
        odd_imag = state[imag, lanes:]
        for rows, cols, value in (
            (real, slice(0, lanes), p * even_real + q * odd_imag),
            (imag, slice(0, lanes), p * even_imag - q * odd_real),
            (real, slice(lanes, width), p * odd_real - q * even_imag),
            (imag, slice(lanes, width), p * odd_imag + q * even_real),
        ):
            high, low = split(value)
            high_side[rows, cols] = high
            low_side[rows, cols] = low

    def sweep(source):
        for g in range(0, units, group):
            rows = slice(g * unit, (g + group) * unit)
            for u in range(g, g + group):
                weigh(u, source)
            state[rows, :lanes] = start[rows, :lanes] + mul_table(
                high_side[rows, :lanes], low_side[rows, :lanes], even_high[...], even_low[...]
            )
            state[rows, lanes:] = start[rows, lanes:] + mul_table(
                high_side[rows, lanes:], low_side[rows, lanes:], odd_high[...], odd_low[...]
            )

    for i in range(2**NS_ITERS - 2):
        sweep(state if i else start)

    scale = scale_of(scalars, (1, lanes))
    stores = []
    for g in range(0, units, group):
        rows = slice(g * unit, (g + group) * unit)
        for u in range(g, g + group):
            weigh(u, state)
        value = scale * (
            spread[rows, :]
            + mul_table(high_side[rows, :], low_side[rows, :], backward_high[...], backward_low[...])
        )
        spread[rows, :] = value
        here = pl.ds(g * unit, group * unit)
        stores.append(pltpu.make_async_copy(spread.at[here], out.at[here], store_sem.at[g]))
        stores[-1].start()
    for store in stores:
        store.wait()


def output_kernel(
    applied,
    gather_high_far,
    gather_low_far,
    out,
    here,
    gather_high,
    gather_low,
    result,
    fetch_sem,
    store_sem,
):
    columns, y_orders, _, orders = out.shape
    padded = gather_high.shape[0] // 2
    span = gather_high.shape[1]
    kept = min(y_orders, span // 2)
    tables = [
        pltpu.make_async_copy(gather_high_far, gather_high, fetch_sem.at[columns]),
        pltpu.make_async_copy(gather_low_far, gather_low, fetch_sem.at[columns + 1]),
    ]
    fetches = []
    for c in range(columns):
        rows = pl.ds(c * span, span)
        fetches.append(pltpu.make_async_copy(applied.at[rows], here.at[rows], fetch_sem.at[c]))
    for copy in tables + fetches:
        copy.start()
    for copy in tables:
        copy.wait()
    stores = []
    for c in range(columns):
        fetches[c].wait()
        high, low = split(here[c * span : (c + 1) * span, :])
        value = (
            mul(gather_high[...], high) + mul(gather_high[...], low) + mul(gather_low[...], high)
        )
        for part in range(2):
            base = part * padded
            for first in range(0, y_orders, kept):
                size = min(kept, y_orders - first)
                result[c, first : first + size, part, :] = value[base : base + size, :orders]
        stores.append(pltpu.make_async_copy(result.at[c], out.at[c], store_sem.at[c]))
        stores[-1].start()
    for store in stores:
        store.wait()


def local(pixel_map, materials, mode_panel):
    rows, pixels = pixel_map.shape
    columns, _, y_orders, orders = mode_panel.shape
    devices = lax.axis_size("long")
    lines = rows * devices
    lanes = round_up(orders, 2 * BLOCK)
    width = 2 * lanes
    total = columns * 2 * lines
    symbol_pair = symbol_table(orders, pixels)
    spread_pair, gather_pair = line_tables(y_orders, lines)
    forward, backward, even, odd = order_tables(orders)
    tables = [*spread_pair, *forward, *backward, *even, *odd]
    panel = mode_panel.transpose(0, 2, 1, 3)
    applied = pl.pallas_call(
        apply_kernel,
        out_shape=jax.ShapeDtypeStruct((total, lanes), jnp.float32),
        in_specs=[pl.BlockSpec(memory_space=pl.ANY)] * (5 + len(tables)),
        out_specs=pl.BlockSpec(memory_space=pl.ANY),
        scratch_shapes=[
            pltpu.SMEM(materials.shape, jnp.float32),
            pltpu.VMEM(pixel_map.shape, jnp.int32),
            pltpu.VMEM(panel.shape, jnp.float32),
            *[pltpu.VMEM(table.shape, jnp.bfloat16) for table in tables],
            pltpu.VMEM((pixels, width), jnp.bfloat16),
            pltpu.VMEM((pixels, width), jnp.bfloat16),
            pltpu.VMEM((lines, width), jnp.float32),
            pltpu.VMEM((columns, spread_pair[0].shape[1], lanes), jnp.float32),
            pltpu.VMEM((total, lanes), jnp.float32),
            pltpu.VMEM((total, width), jnp.float32),
            pltpu.VMEM((total, width), jnp.float32),
            pltpu.VMEM((total, width), jnp.bfloat16),
            pltpu.VMEM((total, width), jnp.bfloat16),
            pltpu.SemaphoreType.DMA((2 * CHUNKS + 3 + len(tables),)),
            pltpu.SemaphoreType.DMA((devices,)),
            pltpu.SemaphoreType.DMA((devices,)),
            pltpu.SemaphoreType.DMA((total // (2 * BLOCK),)),
        ],
        compiler_params=pltpu.CompilerParams(
            vmem_limit_bytes=VMEM_BYTES, collective_id=0, has_side_effects=True
        ),
        name="apply",
    )(materials, pixel_map, panel, *map(jnp.asarray, tables), *map(jnp.asarray, symbol_pair))
    result = pl.pallas_call(
        output_kernel,
        out_shape=jax.ShapeDtypeStruct(panel.shape, jnp.float32),
        in_specs=[pl.BlockSpec(memory_space=pl.ANY)] * 3,
        out_specs=pl.BlockSpec(memory_space=pl.ANY),
        scratch_shapes=[
            pltpu.VMEM((total, lanes), jnp.float32),
            *[pltpu.VMEM(table.shape, jnp.bfloat16) for table in gather_pair],
            pltpu.VMEM(panel.shape, jnp.float32),
            pltpu.SemaphoreType.DMA((columns + 2,)),
            pltpu.SemaphoreType.DMA((columns,)),
        ],
        compiler_params=pltpu.CompilerParams(vmem_limit_bytes=VMEM_BYTES),
        name="output",
    )(applied, *map(jnp.asarray, gather_pair))
    return result.transpose(0, 2, 1, 3)


def solution(mesh):
    in_specs = (P(("grp", "long"), None), P("grp"), P(("grp", "long"), None, None, None))
    out_specs = P(("grp", "long"), None, None, None)
    return jax.shard_map(local, mesh=mesh, in_specs=in_specs, out_specs=out_specs, check_vma=False)
```

```python
import functools

import jax
import jax.numpy as jnp
import ml_dtypes
import numpy as np
from jax import lax
from jax.experimental import pallas as pl
from jax.experimental.pallas import tpu as pltpu
from jax.sharding import PartitionSpec as P

NS_ITERS = 3
BLOCK = 128
CHUNKS = 4
VMEM_BYTES = 62 * 1024 * 1024


def round_up(value, step):
    return -(-value // step) * step


def split_table(table):
    high = table.astype(np.float32).astype(ml_dtypes.bfloat16)
    low = (table - high.astype(np.float64)).astype(ml_dtypes.bfloat16)
    return high, low


def turns(first, second, period):
    return np.mod(np.outer(first, second), period) * (2.0 * np.pi / period)


def symbol_table(orders, pixels):
    reach = orders - 1
    period = 2 * orders - 1
    lanes = round_up(orders, 2 * BLOCK)
    harmonics = np.arange(1, reach + 1)
    frequencies = np.arange(orders)
    by_frequency = turns(harmonics, frequencies, period)
    by_pixel = turns(np.arange(pixels), harmonics, pixels)
    table = np.zeros((pixels, 2 * lanes))
    table[:, :orders] = (1.0 + 2.0 * np.cos(by_pixel) @ np.cos(by_frequency)) / pixels
    table[:, lanes : lanes + orders] = -2.0 * np.sin(by_pixel) @ np.sin(by_frequency) / pixels
    return split_table(table)


def order_tables(orders):
    period = 2 * orders - 1
    lanes = round_up(orders, 2 * BLOCK)
    angle = turns(np.arange(orders) - (orders - 1) // 2, np.arange(orders), period)
    weight = np.where(np.arange(orders) == 0, 1.0, 2.0)[:, None] / period
    forward = np.zeros((lanes, 2 * lanes))
    forward[:orders, :orders] = np.cos(angle)
    forward[:orders, lanes : lanes + orders] = np.sin(angle)
    backward = np.zeros((2 * lanes, lanes))
    backward[:orders, :orders] = weight * np.cos(angle).T
    backward[lanes : lanes + orders, :orders] = weight * np.sin(angle).T
    even = backward[:lanes] @ forward[:, :lanes]
    odd = backward[lanes:] @ forward[:, lanes:]
    return split_table(forward), split_table(backward), split_table(even), split_table(odd)


def line_tables(y_orders, lines, block):
    kept = min(y_orders, lines)
    padded = round_up(kept, BLOCK)
    blocks = lines // block
    angle = turns(np.arange(lines), np.arange(kept) - (y_orders - 1) // 2, lines)
    cosine = np.zeros((blocks, block, padded))
    sine = np.zeros((blocks, block, padded))
    cosine[:, :, :kept] = np.cos(angle).reshape(blocks, block, kept)
    sine[:, :, :kept] = np.sin(angle).reshape(blocks, block, kept)
    real = np.concatenate([cosine, -sine], axis=2)
    imag = np.concatenate([sine, cosine], axis=2)
    spread = np.stack([real, imag], axis=1).reshape(2 * lines, 2 * padded)
    return split_table(spread), split_table(spread.T / lines)


def split(value):
    high = value.astype(jnp.bfloat16)
    return high, (value - high.astype(jnp.float32)).astype(jnp.bfloat16)


def mul(left, right):
    return jnp.dot(left, right, preferred_element_type=jnp.float32)


def mul_table(high, low, table_high, table_low):
    return mul(high, table_high) + mul(low, table_high) + mul(high, table_low)


def scale_of(materials, shape):
    values = [jnp.full(shape, materials[i], jnp.float32) for i in range(materials.shape[0])]
    least = functools.reduce(jnp.minimum, values)
    most = functools.reduce(jnp.maximum, values)
    return 2.0 / (1.0 / least + 1.0 / most)


def symbol_of(materials, pixels, tables, fetched, sums):
    inverse_eps = jnp.zeros(pixels.shape, jnp.float32)
    for i in range(materials.shape[0]):
        inverse = 1.0 / jnp.full(pixels.shape, materials[i], jnp.float32)
        inverse_eps = jnp.where(pixels == i, inverse, inverse_eps)
    high, low = split(inverse_eps)
    rows = jnp.concatenate([high, low], axis=0)
    count = pixels.shape[0]
    total = jnp.zeros((2 * count, tables[0].shape[1]), jnp.float32)
    depth = rows.shape[1] // len(fetched)
    for i, copies in enumerate(fetched):
        part = slice(i * depth, (i + 1) * depth)
        for copy, table in zip(copies, tables):
            copy.wait()
            total += mul(rows[:, part], table[part, :])
    total = total[:count] + total[count:]
    lanes = total.shape[1] // 2
    scaled = scale_of(materials, total.shape) * total
    sums[:, :lanes] = 1.0 - scaled[:, :lanes]
    sums[:, lanes:] = -scaled[:, lanes:]


def apply_kernel(
    materials,
    pixel_rows,
    panel,
    spread_high,
    spread_low,
    forward_high,
    forward_low,
    backward_high_far,
    backward_low_far,
    even_high_far,
    even_low_far,
    odd_high_far,
    odd_low_far,
    table_high,
    table_low,
    out,
    scalars,
    pixels,
    panel_here,
    spread_high_here,
    spread_low_here,
    forward_high_here,
    forward_low_here,
    backward_high,
    backward_low,
    even_high,
    even_low,
    odd_high,
    odd_low,
    high_table,
    low_table,
    landed,
    folded,
    spread,
    start,
    state,
    high_side,
    low_side,
    fetch_sem,
    send_sem,
    recv_sem,
    store_sem,
):
    sources = (
        (materials, scalars),
        (pixel_rows, pixels),
        (panel, panel_here),
        (spread_high, spread_high_here),
        (spread_low, spread_low_here),
        (forward_high, forward_high_here),
        (forward_low, forward_low_here),
        (backward_high_far, backward_high),
        (backward_low_far, backward_low),
        (even_high_far, even_high),
        (even_low_far, even_low),
        (odd_high_far, odd_high),
        (odd_low_far, odd_low),
    )
    fetches = [
        pltpu.make_async_copy(source, target, fetch_sem.at[2 * CHUNKS + i])
        for i, (source, target) in enumerate(sources)
    ]
    early, late = fetches[:7], fetches[7:]
    for copy in early[:2]:
        copy.start()
    me = lax.axis_index("long")
    devices = lax.axis_size("long")
    barrier = pltpu.get_barrier_semaphore()
    for i in range(1, devices):
        pl.semaphore_signal(barrier, inc=1, device_id={"long": lax.rem(me + i, devices)})
    depth = table_high.shape[0] // CHUNKS
    fetched = []
    for i in range(CHUNKS):
        part = pl.ds(i * depth, depth)
        copies = [
            pltpu.make_async_copy(source.at[part], target.at[part], fetch_sem.at[2 * i + j])
            for j, (source, target) in enumerate(((table_high, high_table), (table_low, low_table)))
        ]
        for copy in copies:
            copy.start()
        fetched.append(copies)
    for copy in early[2:] + late:
        copy.start()
    count = pixels.shape[0]

    def slot(device):
        return landed.at[pl.ds(pl.multiple_of(device * count, count), count)]

    def send(device, i):
        return pltpu.make_async_remote_copy(
            src_ref=slot(device),
            dst_ref=slot(device),
            send_sem=send_sem.at[i],
            recv_sem=recv_sem.at[device],
            device_id={"long": lax.rem(me + i, devices)},
        )

    mine = slot(me)
    for copy in early[:2]:
        copy.wait()
    symbol_of(scalars, pixels[...], (high_table, low_table), fetched, mine)
    pl.semaphore_wait(barrier, devices - 1)
    sent = [send(me, i) for i in range(1, devices)]
    for copy in sent:
        copy.start()

    columns, y_orders, _, orders = panel.shape
    lines = landed.shape[0]
    kept = min(y_orders, lines)
    padded = spread_high.shape[1] // 2
    block = BLOCK // columns
    blocks = lines // block
    unit = 2 * BLOCK
    folded[...] = jnp.zeros(folded.shape, jnp.float32)
    for copy in early[2:]:
        copy.wait()
    for c in range(columns):
        for part in range(2):
            base = part * padded
            folded[c, base : base + kept, :orders] = panel_here[c, :kept, part, :]
            for first in range(kept, y_orders, kept):
                size = min(kept, y_orders - first)
                folded[c, base : base + size, :orders] += panel_here[c, first : first + size, part, :]
        high, low = split(folded[c])
        value = (
            mul(spread_high_here[...], high)
            + mul(spread_high_here[...], low)
            + mul(spread_low_here[...], high)
        )
        high, low = split(value)
        begun = mul_table(high, low, forward_high_here[...], forward_low_here[...])
        for b in range(blocks):
            rows = slice(b * unit + c * 2 * block, b * unit + (c + 1) * 2 * block)
            spread[rows, :] = value[b * 2 * block : (b + 1) * 2 * block, :]
            start[rows, :] = begun[b * 2 * block : (b + 1) * 2 * block, :]

    symbol = landed
    for copy in late:
        copy.wait()

    width = symbol.shape[1]
    lanes = width // 2
    group = 2 if blocks % 2 == 0 else 1
    scale = scale_of(scalars, (1, lanes))

    def weigh(b, state):
        here = slice(b * block, (b + 1) * block)
        p = symbol[here, :lanes]
        q = symbol[here, lanes:]
        for c in range(columns):
            first = b * unit + c * 2 * block
            real = slice(first, first + block)
            imag = slice(first + block, first + 2 * block)
            even_real = state[real, :lanes]
            even_imag = state[imag, :lanes]
            odd_real = state[real, lanes:]
            odd_imag = state[imag, lanes:]
            for rows, cols, value in (
                (real, slice(0, lanes), p * even_real + q * odd_imag),
                (imag, slice(0, lanes), p * even_imag - q * odd_real),
                (real, slice(lanes, width), p * odd_real - q * even_imag),
                (imag, slice(lanes, width), p * odd_imag + q * even_real),
            ):
                high, low = split(value)
                high_side[rows, cols] = high
                low_side[rows, cols] = low

    def sweep(b, source):
        weigh(b, source)
        rows = slice(b * unit, (b + 1) * unit)
        state[rows, :lanes] = start[rows, :lanes] + mul_table(
            high_side[rows, :lanes], low_side[rows, :lanes], even_high[...], even_low[...]
        )
        state[rows, lanes:] = start[rows, lanes:] + mul_table(
            high_side[rows, lanes:], low_side[rows, lanes:], odd_high[...], odd_low[...]
        )

    def arrive(device):
        @pl.when(device != me)
        def _():
            send(device, 1).wait_recv()

    stores = []
    arrived = 0
    for g in range(0, blocks, group):
        while arrived * count < (g + group) * block:
            arrive(arrived)
            arrived += 1
        for i in range(2**NS_ITERS - 2):
            for b in range(g, g + group):
                sweep(b, state if i else start)
        for b in range(g, g + group):
            weigh(b, state)
            rows = slice(b * unit, (b + 1) * unit)
            spread[rows, :] = scale * (
                spread[rows, :]
                + mul_table(
                    high_side[rows, :], low_side[rows, :], backward_high[...], backward_low[...]
                )
            )
            here = pl.ds(b * unit, unit)
            stores.append(pltpu.make_async_copy(spread.at[here], out.at[here], store_sem.at[b]))
            stores[-1].start()
    for copy in sent:
        copy.wait_send()
    for store in stores:
        store.wait()


def output_kernel(
    applied,
    gather_high_far,
    gather_low_far,
    out,
    here,
    gather_high,
    gather_low,
    result,
    fetch_sem,
    store_sem,
):
    columns, y_orders, _, orders = out.shape
    padded = gather_high.shape[0] // 2
    span = gather_high.shape[1]
    kept = min(y_orders, span // 2)
    block = BLOCK // columns
    blocks = span // (2 * block)
    unit = 2 * BLOCK
    tables = [
        pltpu.make_async_copy(gather_high_far, gather_high, fetch_sem.at[blocks]),
        pltpu.make_async_copy(gather_low_far, gather_low, fetch_sem.at[blocks + 1]),
    ]
    fetches = []
    for b in range(blocks):
        rows = pl.ds(b * unit, unit)
        fetches.append(pltpu.make_async_copy(applied.at[rows], here.at[rows], fetch_sem.at[b]))
    for copy in tables + fetches:
        copy.start()
    for copy in tables + fetches:
        copy.wait()
    stores = []
    for c in range(columns):
        first = c * 2 * block
        pieces = [here[b * unit + first : b * unit + first + 2 * block, :] for b in range(blocks)]
        high, low = split(jnp.concatenate(pieces, axis=0))
        value = (
            mul(gather_high[...], high) + mul(gather_high[...], low) + mul(gather_low[...], high)
        )
        for part in range(2):
            base = part * padded
            for first in range(0, y_orders, kept):
                size = min(kept, y_orders - first)
                result[c, first : first + size, part, :] = value[base : base + size, :orders]
        stores.append(pltpu.make_async_copy(result.at[c], out.at[c], store_sem.at[c]))
        stores[-1].start()
    for store in stores:
        store.wait()


def local(pixel_map, materials, mode_panel):
    rows, pixels = pixel_map.shape
    columns, _, y_orders, orders = mode_panel.shape
    devices = lax.axis_size("long")
    lines = rows * devices
    lanes = round_up(orders, 2 * BLOCK)
    width = 2 * lanes
    total = columns * 2 * lines
    symbol_pair = symbol_table(orders, pixels)
    spread_pair, gather_pair = line_tables(y_orders, lines, BLOCK // columns)
    forward, backward, even, odd = order_tables(orders)
    tables = [*spread_pair, *forward, *backward, *even, *odd]
    panel = mode_panel.transpose(0, 2, 1, 3)
    applied = pl.pallas_call(
        apply_kernel,
        out_shape=jax.ShapeDtypeStruct((total, lanes), jnp.float32),
        in_specs=[pl.BlockSpec(memory_space=pl.ANY)] * (5 + len(tables)),
        out_specs=pl.BlockSpec(memory_space=pl.ANY),
        scratch_shapes=[
            pltpu.SMEM(materials.shape, jnp.float32),
            pltpu.VMEM(pixel_map.shape, jnp.int32),
            pltpu.VMEM(panel.shape, jnp.float32),
            *[pltpu.VMEM(table.shape, jnp.bfloat16) for table in tables],
            pltpu.VMEM((pixels, width), jnp.bfloat16),
            pltpu.VMEM((pixels, width), jnp.bfloat16),
            pltpu.VMEM((lines, width), jnp.float32),
            pltpu.VMEM((columns, spread_pair[0].shape[1], lanes), jnp.float32),
            pltpu.VMEM((total, lanes), jnp.float32),
            pltpu.VMEM((total, width), jnp.float32),
            pltpu.VMEM((total, width), jnp.float32),
            pltpu.VMEM((total, width), jnp.bfloat16),
            pltpu.VMEM((total, width), jnp.bfloat16),
            pltpu.SemaphoreType.DMA((2 * CHUNKS + 3 + len(tables),)),
            pltpu.SemaphoreType.DMA((devices,)),
            pltpu.SemaphoreType.DMA((devices,)),
            pltpu.SemaphoreType.DMA((total // (2 * BLOCK),)),
        ],
        compiler_params=pltpu.CompilerParams(
            vmem_limit_bytes=VMEM_BYTES, collective_id=0, has_side_effects=True
        ),
        name="apply",
    )(materials, pixel_map, panel, *map(jnp.asarray, tables), *map(jnp.asarray, symbol_pair))
    result = pl.pallas_call(
        output_kernel,
        out_shape=jax.ShapeDtypeStruct(panel.shape, jnp.float32),
        in_specs=[pl.BlockSpec(memory_space=pl.ANY)] * 3,
        out_specs=pl.BlockSpec(memory_space=pl.ANY),
        scratch_shapes=[
            pltpu.VMEM((total, lanes), jnp.float32),
            *[pltpu.VMEM(table.shape, jnp.bfloat16) for table in gather_pair],
            pltpu.VMEM(panel.shape, jnp.float32),
            pltpu.SemaphoreType.DMA((total // (2 * BLOCK) + 2,)),
            pltpu.SemaphoreType.DMA((columns,)),
        ],
        compiler_params=pltpu.CompilerParams(vmem_limit_bytes=VMEM_BYTES),
        name="output",
    )(applied, *map(jnp.asarray, gather_pair))
    return result.transpose(0, 2, 1, 3)


def solution(mesh):
    in_specs = (P(("grp", "long"), None), P("grp"), P(("grp", "long"), None, None, None))
    out_specs = P(("grp", "long"), None, None, None)
    return jax.shard_map(local, mesh=mesh, in_specs=in_specs, out_specs=out_specs, check_vma=False)
```

```python
import functools

import jax
import jax.numpy as jnp
import ml_dtypes
import numpy as np
from jax import lax
from jax.experimental import pallas as pl
from jax.experimental.pallas import tpu as pltpu
from jax.sharding import PartitionSpec as P

NS_ITERS = 3
BLOCK = 128
CHUNKS = 4
VMEM_BYTES = 62 * 1024 * 1024


def round_up(value, step):
    return -(-value // step) * step


def split_table(table):
    high = table.astype(np.float32).astype(ml_dtypes.bfloat16)
    low = (table - high.astype(np.float64)).astype(ml_dtypes.bfloat16)
    return high, low


def turns(first, second, period):
    return np.mod(np.outer(first, second), period) * (2.0 * np.pi / period)


def symbol_table(orders, pixels):
    reach = orders - 1
    period = 2 * orders - 1
    lanes = round_up(orders, 2 * BLOCK)
    harmonics = np.arange(1, reach + 1)
    frequencies = np.arange(orders)
    by_frequency = turns(harmonics, frequencies, period)
    by_pixel = turns(np.arange(pixels), harmonics, pixels)
    table = np.zeros((pixels, 2 * lanes))
    table[:, :orders] = (1.0 + 2.0 * np.cos(by_pixel) @ np.cos(by_frequency)) / pixels
    table[:, lanes : lanes + orders] = -2.0 * np.sin(by_pixel) @ np.sin(by_frequency) / pixels
    return split_table(table)


def order_tables(orders):
    period = 2 * orders - 1
    lanes = round_up(orders, 2 * BLOCK)
    angle = turns(np.arange(orders) - (orders - 1) // 2, np.arange(orders), period)
    weight = np.where(np.arange(orders) == 0, 1.0, 2.0)[:, None] / period
    forward = np.zeros((lanes, 2 * lanes))
    forward[:orders, :orders] = np.cos(angle)
    forward[:orders, lanes : lanes + orders] = np.sin(angle)
    backward = np.zeros((2 * lanes, lanes))
    backward[:orders, :orders] = weight * np.cos(angle).T
    backward[lanes : lanes + orders, :orders] = weight * np.sin(angle).T
    even = backward[:lanes] @ forward[:, :lanes]
    odd = backward[lanes:] @ forward[:, lanes:]
    return split_table(forward), split_table(backward), split_table(even), split_table(odd)


def line_tables(y_orders, lines, block):
    kept = min(y_orders, lines)
    padded = round_up(kept, BLOCK)
    blocks = lines // block
    angle = turns(np.arange(lines), np.arange(kept) - (y_orders - 1) // 2, lines)
    cosine = np.zeros((blocks, block, padded))
    sine = np.zeros((blocks, block, padded))
    cosine[:, :, :kept] = np.cos(angle).reshape(blocks, block, kept)
    sine[:, :, :kept] = np.sin(angle).reshape(blocks, block, kept)
    real = np.concatenate([cosine, -sine], axis=2)
    imag = np.concatenate([sine, cosine], axis=2)
    spread = np.stack([real, imag], axis=1).reshape(2 * lines, 2 * padded)
    return split_table(spread), split_table(spread.T / lines)


def split(value):
    high = value.astype(jnp.bfloat16)
    return high, (value - high.astype(jnp.float32)).astype(jnp.bfloat16)


def mul(left, right):
    return jnp.dot(left, right, preferred_element_type=jnp.float32)


def mul_table(high, low, table_high, table_low):
    return mul(high, table_high) + mul(low, table_high) + mul(high, table_low)


def scale_of(materials, shape):
    values = [jnp.full(shape, materials[i], jnp.float32) for i in range(materials.shape[0])]
    least = functools.reduce(jnp.minimum, values)
    most = functools.reduce(jnp.maximum, values)
    return 2.0 / (1.0 / least + 1.0 / most)


def symbol_of(materials, pixels, tables, fetched, sums):
    inverse_eps = jnp.zeros(pixels.shape, jnp.float32)
    for i in range(materials.shape[0]):
        inverse = 1.0 / jnp.full(pixels.shape, materials[i], jnp.float32)
        inverse_eps = jnp.where(pixels == i, inverse, inverse_eps)
    high, low = split(inverse_eps)
    rows = jnp.concatenate([high, low], axis=0)
    count = pixels.shape[0]
    total = jnp.zeros((2 * count, tables[0].shape[1]), jnp.float32)
    depth = rows.shape[1] // len(fetched)
    for i, copies in enumerate(fetched):
        part = slice(i * depth, (i + 1) * depth)
        for copy, table in zip(copies, tables):
            copy.wait()
            total += mul(rows[:, part], table[part, :])
    total = total[:count] + total[count:]
    lanes = total.shape[1] // 2
    scaled = scale_of(materials, total.shape) * total
    sums[:, :lanes] = 1.0 - scaled[:, :lanes]
    sums[:, lanes:] = -scaled[:, lanes:]


def apply_kernel(
    materials,
    pixel_rows,
    panel,
    spread_high,
    spread_low,
    forward_high,
    forward_low,
    backward_high_far,
    backward_low_far,
    even_high_far,
    even_low_far,
    odd_high_far,
    odd_low_far,
    table_high,
    table_low,
    out,
    scalars,
    pixels,
    panel_here,
    spread_high_here,
    spread_low_here,
    forward_high_here,
    forward_low_here,
    backward_high,
    backward_low,
    even_high,
    even_low,
    odd_high,
    odd_low,
    high_table,
    low_table,
    landed,
    folded,
    spread,
    start,
    state,
    high_side,
    low_side,
    fetch_sem,
    send_sem,
    recv_sem,
    store_sem,
):
    sources = (
        (materials, scalars),
        (pixel_rows, pixels),
        (panel, panel_here),
        (spread_high, spread_high_here),
        (spread_low, spread_low_here),
        (forward_high, forward_high_here),
        (forward_low, forward_low_here),
        (backward_high_far, backward_high),
        (backward_low_far, backward_low),
        (even_high_far, even_high),
        (even_low_far, even_low),
        (odd_high_far, odd_high),
        (odd_low_far, odd_low),
    )
    fetches = [
        pltpu.make_async_copy(source, target, fetch_sem.at[2 * CHUNKS + i])
        for i, (source, target) in enumerate(sources)
    ]
    early, late = fetches[:7], fetches[7:]
    for copy in early[:2]:
        copy.start()
    me = lax.axis_index("long")
    devices = lax.axis_size("long")
    barrier = pltpu.get_barrier_semaphore()
    for i in range(1, devices):
        pl.semaphore_signal(barrier, inc=1, device_id={"long": lax.rem(me + i, devices)})
    depth = table_high.shape[0] // CHUNKS
    fetched = []
    for i in range(CHUNKS):
        part = pl.ds(i * depth, depth)
        copies = [
            pltpu.make_async_copy(source.at[part], target.at[part], fetch_sem.at[2 * i + j])
            for j, (source, target) in enumerate(((table_high, high_table), (table_low, low_table)))
        ]
        for copy in copies:
            copy.start()
        fetched.append(copies)
    for copy in early[2:] + late:
        copy.start()
    count = pixels.shape[0]

    def slot(device):
        return landed.at[pl.ds(pl.multiple_of(device * count, count), count)]

    def send(device, i):
        return pltpu.make_async_remote_copy(
            src_ref=slot(device),
            dst_ref=slot(device),
            send_sem=send_sem.at[i],
            recv_sem=recv_sem.at[device],
            device_id={"long": lax.rem(me + i, devices)},
        )

    mine = slot(me)
    for copy in early[:2]:
        copy.wait()
    symbol_of(scalars, pixels[...], (high_table, low_table), fetched, mine)
    pl.semaphore_wait(barrier, devices - 1)
    sent = [send(me, i) for i in range(1, devices)]
    for copy in sent:
        copy.start()

    columns, y_orders, _, orders = panel.shape
    lines = landed.shape[0]
    kept = min(y_orders, lines)
    padded = spread_high.shape[1] // 2
    block = BLOCK // columns
    blocks = lines // block
    unit = 2 * BLOCK
    folded[...] = jnp.zeros(folded.shape, jnp.float32)
    for copy in early[2:]:
        copy.wait()
    for c in range(columns):
        for part in range(2):
            base = part * padded
            folded[c, base : base + kept, :orders] = panel_here[c, :kept, part, :]
            for first in range(kept, y_orders, kept):
                size = min(kept, y_orders - first)
                folded[c, base : base + size, :orders] += panel_here[c, first : first + size, part, :]
        high, low = split(folded[c])
        value = (
            mul(spread_high_here[...], high)
            + mul(spread_high_here[...], low)
            + mul(spread_low_here[...], high)
        )
        high, low = split(value)
        begun = mul_table(high, low, forward_high_here[...], forward_low_here[...])
        for b in range(blocks):
            rows = slice(b * unit + c * 2 * block, b * unit + (c + 1) * 2 * block)
            spread[rows, :] = value[b * 2 * block : (b + 1) * 2 * block, :]
            start[rows, :] = begun[b * 2 * block : (b + 1) * 2 * block, :]

    symbol = landed
    for copy in late:
        copy.wait()

    width = symbol.shape[1]
    lanes = width // 2
    group = 2 if blocks % 2 == 0 else 1
    scale = scale_of(scalars, (1, lanes))

    def weigh(b, state):
        here = slice(b * block, (b + 1) * block)
        p = symbol[here, :lanes]
        q = symbol[here, lanes:]
        for c in range(columns):
            first = b * unit + c * 2 * block
            real = slice(first, first + block)
            imag = slice(first + block, first + 2 * block)
            even_real = state[real, :lanes]
            even_imag = state[imag, :lanes]
            odd_real = state[real, lanes:]
            odd_imag = state[imag, lanes:]
            for rows, cols, value in (
                (real, slice(0, lanes), p * even_real + q * odd_imag),
                (imag, slice(0, lanes), p * even_imag - q * odd_real),
                (real, slice(lanes, width), p * odd_real - q * even_imag),
                (imag, slice(lanes, width), p * odd_imag + q * even_real),
            ):
                high, low = split(value)
                high_side[rows, cols] = high
                low_side[rows, cols] = low

    def sweep(b, source):
        weigh(b, source)
        rows = slice(b * unit, (b + 1) * unit)
        state[rows, :lanes] = start[rows, :lanes] + mul_table(
            high_side[rows, :lanes], low_side[rows, :lanes], even_high[...], even_low[...]
        )
        state[rows, lanes:] = start[rows, lanes:] + mul_table(
            high_side[rows, lanes:], low_side[rows, lanes:], odd_high[...], odd_low[...]
        )

    def arrive(device):
        @pl.when(device != me)
        def _():
            send(device, 1).wait_recv()

    def store(b):
        here = pl.ds(b * unit, unit)
        return pltpu.make_async_copy(spread.at[here], out.at[here], store_sem.at[b])

    def run(g):
        for device in range(g * block // count, (g + group) * block // count):
            arrive(device)
        for i in range(2**NS_ITERS - 2):
            for b in range(g, g + group):
                sweep(b, state if i else start)
        for b in range(g, g + group):
            weigh(b, state)
            rows = slice(b * unit, (b + 1) * unit)
            spread[rows, :] = scale * (
                spread[rows, :]
                + mul_table(
                    high_side[rows, :], low_side[rows, :], backward_high[...], backward_low[...]
                )
            )
            store(b).start()

    lower = me < devices // 2

    @pl.when(lower)
    def _():
        run(0)

    for g in range(group, blocks, group):
        run(g)

    @pl.when(jnp.logical_not(lower))
    def _():
        run(0)

    for copy in sent:
        copy.wait_send()
    for b in range(blocks):
        store(b).wait()


def output_kernel(
    applied,
    gather_high_far,
    gather_low_far,
    out,
    here,
    gather_high,
    gather_low,
    result,
    fetch_sem,
    store_sem,
):
    columns, y_orders, _, orders = out.shape
    padded = gather_high.shape[0] // 2
    span = gather_high.shape[1]
    kept = min(y_orders, span // 2)
    block = BLOCK // columns
    blocks = span // (2 * block)
    unit = 2 * BLOCK
    tables = [
        pltpu.make_async_copy(gather_high_far, gather_high, fetch_sem.at[blocks]),
        pltpu.make_async_copy(gather_low_far, gather_low, fetch_sem.at[blocks + 1]),
    ]
    fetches = []
    for b in range(blocks):
        rows = pl.ds(b * unit, unit)
        fetches.append(pltpu.make_async_copy(applied.at[rows], here.at[rows], fetch_sem.at[b]))
    for copy in tables + fetches:
        copy.start()
    for copy in tables + fetches:
        copy.wait()
    stores = []
    for c in range(columns):
        first = c * 2 * block
        pieces = [here[b * unit + first : b * unit + first + 2 * block, :] for b in range(blocks)]
        high, low = split(jnp.concatenate(pieces, axis=0))
        value = (
            mul(gather_high[...], high) + mul(gather_high[...], low) + mul(gather_low[...], high)
        )
        for part in range(2):
            base = part * padded
            for first in range(0, y_orders, kept):
                size = min(kept, y_orders - first)
                result[c, first : first + size, part, :] = value[base : base + size, :orders]
        stores.append(pltpu.make_async_copy(result.at[c], out.at[c], store_sem.at[c]))
        stores[-1].start()
    for store in stores:
        store.wait()


def local(pixel_map, materials, mode_panel):
    rows, pixels = pixel_map.shape
    columns, _, y_orders, orders = mode_panel.shape
    devices = lax.axis_size("long")
    lines = rows * devices
    lanes = round_up(orders, 2 * BLOCK)
    width = 2 * lanes
    total = columns * 2 * lines
    symbol_pair = symbol_table(orders, pixels)
    spread_pair, gather_pair = line_tables(y_orders, lines, BLOCK // columns)
    forward, backward, even, odd = order_tables(orders)
    tables = [*spread_pair, *forward, *backward, *even, *odd]
    panel = mode_panel.transpose(0, 2, 1, 3)
    applied = pl.pallas_call(
        apply_kernel,
        out_shape=jax.ShapeDtypeStruct((total, lanes), jnp.float32),
        in_specs=[pl.BlockSpec(memory_space=pl.ANY)] * (5 + len(tables)),
        out_specs=pl.BlockSpec(memory_space=pl.ANY),
        scratch_shapes=[
            pltpu.SMEM(materials.shape, jnp.float32),
            pltpu.VMEM(pixel_map.shape, jnp.int32),
            pltpu.VMEM(panel.shape, jnp.float32),
            *[pltpu.VMEM(table.shape, jnp.bfloat16) for table in tables],
            pltpu.VMEM((pixels, width), jnp.bfloat16),
            pltpu.VMEM((pixels, width), jnp.bfloat16),
            pltpu.VMEM((lines, width), jnp.float32),
            pltpu.VMEM((columns, spread_pair[0].shape[1], lanes), jnp.float32),
            pltpu.VMEM((total, lanes), jnp.float32),
            pltpu.VMEM((total, width), jnp.float32),
            pltpu.VMEM((total, width), jnp.float32),
            pltpu.VMEM((total, width), jnp.bfloat16),
            pltpu.VMEM((total, width), jnp.bfloat16),
            pltpu.SemaphoreType.DMA((2 * CHUNKS + 3 + len(tables),)),
            pltpu.SemaphoreType.DMA((devices,)),
            pltpu.SemaphoreType.DMA((devices,)),
            pltpu.SemaphoreType.DMA((total // (2 * BLOCK),)),
        ],
        compiler_params=pltpu.CompilerParams(
            vmem_limit_bytes=VMEM_BYTES, collective_id=0, has_side_effects=True
        ),
        name="apply",
    )(materials, pixel_map, panel, *map(jnp.asarray, tables), *map(jnp.asarray, symbol_pair))
    result = pl.pallas_call(
        output_kernel,
        out_shape=jax.ShapeDtypeStruct(panel.shape, jnp.float32),
        in_specs=[pl.BlockSpec(memory_space=pl.ANY)] * 3,
        out_specs=pl.BlockSpec(memory_space=pl.ANY),
        scratch_shapes=[
            pltpu.VMEM((total, lanes), jnp.float32),
            *[pltpu.VMEM(table.shape, jnp.bfloat16) for table in gather_pair],
            pltpu.VMEM(panel.shape, jnp.float32),
            pltpu.SemaphoreType.DMA((total // (2 * BLOCK) + 2,)),
            pltpu.SemaphoreType.DMA((columns,)),
        ],
        compiler_params=pltpu.CompilerParams(vmem_limit_bytes=VMEM_BYTES),
        name="output",
    )(applied, *map(jnp.asarray, gather_pair))
    return result.transpose(0, 2, 1, 3)


def solution(mesh):
    in_specs = (P(("grp", "long"), None), P("grp"), P(("grp", "long"), None, None, None))
    out_specs = P(("grp", "long"), None, None, None)
    return jax.shard_map(local, mesh=mesh, in_specs=in_specs, out_specs=out_specs, check_vma=False)
```
